128 devices in a mesh: kvh: 4 (over x), seq: 32 (over y, z, core).
Axes of the slice: x: 4, y: 4, z: 4, core: 2. Of those that a mesh axis runs over, the one named last changes fastest.
Arguments:
- queries: bfloat16 [8, 128, 128], P(None, 'kvh'), may hold values from -150 to 150
- key_cache: bfloat16 [8, 8, 4096, 128], P(None, 'kvh', 'seq'), may hold values from -6 to 6
- value_cache: bfloat16 [8, 8, 4096, 128], P(None, 'kvh', 'seq'), may hold values from -6 to 6
- new_keys: bfloat16 [8, 8, 128], P(None, 'kvh'), may hold values from -5 to 5
- new_values: bfloat16 [8, 8, 128], P(None, 'kvh'), may hold values from -6 to 6
- block_fill: int32 [8, 32], P(None, 'seq'), may hold values from 0 to 127, as said below
- new_block: int32 [8], replicated, may hold values from 0 to 31, as said below
- residual: float32 [8, 16384], P(None, ('kvh', 'seq')), may hold values from -5 to 5
- norm_gain: float32 [16384], P(('kvh', 'seq')), may hold values from 0.1 to 1.9
- out_weight: bfloat16 [16384, 16384], P(None, ('kvh', 'seq')), may hold values from -0.046875 to 0.046875
- gate_weight: bfloat16 [26624, 16384], P(('kvh', 'seq')), may hold values from -0.046875 to 0.046875
- up_weight: bfloat16 [26624, 16384], P(('kvh', 'seq')), may hold values from -0.046875 to 0.046875
- down_weight: bfloat16 [26624, 16384], P(('kvh', 'seq')), may hold values from -0.0390625 to 0.0390625
Outputs:
- layer_out: bfloat16 [8, 16384], P(None, ('kvh', 'seq'))
- keys_out: bfloat16 [8, 8, 4096, 128], P(None, 'kvh', 'seq')
- values_out: bfloat16 [8, 8, 4096, 128], P(None, 'kvh', 'seq')
The draws below stay inside these ranges and needn't reach their ends.
Inputs may be any that keep to these rules, and one draw needn't show every extreme that they name: `block_fill`: the new row of a request goes to the row of its block just after the rows in use. `new_block`: the first min(8, 32) requests send their new rows to different blocks.
All inputs are finite; a program needn't handle non-finite values.
Results may differ from the reference program's by a relative error of at most 0.0075.
Values may be sent and summed in bfloat16 or wider, within the bound.
No kernel may reach another device: no remote copies, remote signals or barrier semaphores. Data moves between devices by JAX's collectives and lax.ppermute only.
A program may use at most 128 MiB of HBM per device.

```python
import jax
import jax.numpy as jnp
from jax import lax

D = 16384
HQ = 128
KVH = 8
HD = 128
FF = 26624
B = 8
CTX_DEV = 128
BLOCKS = 32
CONTEXT = 4096


def shared_keys(key):
    return jnp.clip(jax.random.normal(jax.random.fold_in(key, 100), (B, KVH, HD), jnp.float32), -5.0, 5.0)


def draw_new_keys(key, part):
    return shared_keys(key).astype(jnp.bfloat16)


def draw_queries(key, part):
    key = jax.random.fold_in(key, 1)
    key_drawn = jax.random.fold_in(key, 0)
    drawn = jnp.clip(2.5 * jax.random.normal(key_drawn, (B, HQ, HD), jnp.float32), -15.0, 15.0)
    return drawn.astype(jnp.bfloat16)


def draw_residual(key, part):
    key = jax.random.fold_in(key, 2)
    key_main = jax.random.fold_in(key, 0)
    column_scale = 0.3 * 3.0 ** (jnp.arange(D, dtype=jnp.float32) / D)
    values = jnp.clip(jax.random.normal(key_main, (B, D), jnp.float32), -5.0, 5.0)
    return jnp.clip(values * column_scale[None, :], -5.0, 5.0)


def draw_block_fill(key, part):
    key = jax.random.fold_in(key, 3)
    fills = jax.random.randint(key, (B, BLOCKS), 0, CTX_DEV, jnp.int32)
    fills = fills.at[0, 0].set(CTX_DEV - 1)
    return fills.at[B - 1, BLOCKS - 1].set(0)


def draw_new_block(key, part):
    key = jax.random.fold_in(key, 4)
    key_perm, key_rest = jax.random.split(key)
    order = jax.random.permutation(key_perm, BLOCKS).astype(jnp.int32)
    rest = jax.random.randint(key_rest, (B,), 0, BLOCKS, jnp.int32)
    index = jnp.arange(B, dtype=jnp.int32)
    leading = order[index % BLOCKS]
    return jnp.where(index < BLOCKS, leading, rest).astype(jnp.int32)


def levels(key, dims, pieces, least, high):
    level = 1.0
    for axis_at, parts in pieces:
        heights = jax.random.uniform(jax.random.fold_in(jax.random.fold_in(key, 6), axis_at), (parts,), jnp.float32, least / len(pieces), high / len(pieces))
        level = level * jnp.repeat(jnp.exp(heights), dims[axis_at] // parts).reshape((-1,) + (1,) * (len(dims) - 1 - axis_at))
    return level


def gaussian(rng, extent, width, reach, cuts=(), kind=jnp.bfloat16):
    loudness = levels(rng, extent, cuts, -0.22, 0.18) if cuts else 1.0
    drawn = jax.random.normal(rng, extent, jnp.float32) * width * loudness
    return jnp.minimum(jnp.maximum(drawn, -reach), reach).astype(kind)


def setup_inputs(seed: int = 0) -> dict:
    key_of = jax.random.split(jax.random.key(seed), 14)
    queries = draw_queries(jax.random.fold_in(key_of[13], 71), 0)
    key_cache = gaussian(key_of[1], (B, KVH, CONTEXT, HD), 1.0, 6.0, ((1, 4), (2, 32)))
    value_cache = gaussian(key_of[2], (B, KVH, CONTEXT, HD), 1.0, 6.0, ((1, 4), (2, 32)))
    new_keys = draw_new_keys(jax.random.fold_in(key_of[13], 71), 0)
    new_values = gaussian(key_of[4], (B, KVH, HD), 1.0, 6.0, ((1, 4),))
    block_fill = draw_block_fill(jax.random.fold_in(key_of[13], 71), 0)
    new_block = draw_new_block(jax.random.fold_in(key_of[13], 71), 0)
    residual = draw_residual(jax.random.fold_in(key_of[13], 71), 0)
    norm_gain = jnp.clip(1.0 + 0.18 * jax.random.normal(key_of[8], (D,), jnp.float32), 0.1, 1.9)
    out_weight = gaussian(key_of[9], (HQ * HD, D), (HQ * HD) ** -0.5, 0.046875, ((1, 128),))
    gate_weight = gaussian(key_of[10], (FF, D), D ** -0.5, 0.046875, ((0, 128),))
    up_weight = gaussian(key_of[11], (FF, D), D ** -0.5, 0.046875, ((0, 128),))
    down_weight = gaussian(key_of[12], (FF, D), FF ** -0.5, 0.0390625, ((0, 128),))
    return dict(queries=queries, key_cache=key_cache, value_cache=value_cache, new_keys=new_keys, new_values=new_values, block_fill=block_fill, new_block=new_block, residual=residual, norm_gain=norm_gain, out_weight=out_weight, gate_weight=gate_weight, up_weight=up_weight, down_weight=down_weight)


def project_rows(normed, weight):
    return lax.dot_general(normed, weight, (((1,), (1,)), ((), ())), preferred_element_type=jnp.float32)

def reference(queries, key_cache, value_cache, new_keys, new_values, block_fill, new_block, residual, norm_gain, out_weight, gate_weight, up_weight, down_weight):
    heads_per = HQ // KVH
    position = jnp.arange(CONTEXT, dtype=jnp.int32)
    block_of = (position // CTX_DEV).astype(jnp.int32)
    row_of = position % CTX_DEV
    fill_at = block_fill[:, block_of]
    chosen_fill = jnp.take_along_axis(block_fill, new_block[:, None].astype(jnp.int32), axis=1)[:, 0]
    target = new_block * CTX_DEV + chosen_fill
    fresh = position[None, :] == target[:, None]
    live = (row_of[None, :] < fill_at) | fresh
    keys_out = jnp.where(fresh[:, None, :, None], new_keys[:, :, None, :], key_cache)
    values_out = jnp.where(fresh[:, None, :, None], new_values[:, :, None, :], value_cache)
    grouped = queries.astype(jnp.float32).reshape(B, KVH, heads_per, HD)
    scores = jnp.einsum('bkgd,bktd->bkgt', grouped, keys_out.astype(jnp.float32), precision=lax.Precision.HIGHEST) * HD ** (-0.5)
    mask = live[:, None, None, :]
    top = lax.optimization_barrier(jnp.max(jnp.where(mask, scores, -1e+30), axis=-1, keepdims=True))
    weights = jnp.where(mask, jnp.exp(jnp.where(mask, scores, top) - top), 0.0)
    total = lax.optimization_barrier(jnp.sum(weights, axis=-1))
    summed = jnp.einsum('bkgt,bktd->bkgd', weights, values_out.astype(jnp.float32), precision=lax.Precision.HIGHEST)
    heads = (summed / total[..., None]).astype(jnp.bfloat16).reshape(B, HQ * HD)
    mixed = residual + jnp.dot(heads, out_weight, preferred_element_type=jnp.float32)
    mean_square = lax.optimization_barrier(jnp.mean(mixed * mixed, axis=1))
    normed = (mixed * lax.rsqrt(mean_square + 1e-05)[:, None] * norm_gain[None, :]).astype(jnp.bfloat16)
    gate = project_rows(normed, gate_weight)
    up_sum = project_rows(normed, up_weight)
    hidden = (jax.nn.silu(gate) * up_sum).astype(jnp.bfloat16)
    layer_out = (mixed + jnp.dot(hidden, down_weight, preferred_element_type=jnp.float32)).astype(jnp.bfloat16)
    return (layer_out, keys_out, values_out)
```

```python
import functools

import jax
import jax.numpy as jnp
from jax import lax
from jax.experimental import pallas as pl
from jax.experimental.pallas import tpu as pltpu
from jax.sharding import PartitionSpec as P

F32 = jnp.float32
BF16 = jnp.bfloat16
EVERY = ("kvh", "seq")
VMEM = pl.BlockSpec(memory_space=pltpu.VMEM)
SMEM = pl.BlockSpec(memory_space=pltpu.SMEM)
ANY = pl.BlockSpec(memory_space=pl.ANY)
MIB = 1 << 20
CHUNK = 2048


def nt_dot(a, b):
    return lax.dot_general(a, b, (((1,), (1,)), ((), ())), preferred_element_type=F32)


def attention_kernel(
    new_block, fill, queries, keys, values, new_keys, new_values, keys_out, values_out, payload, rows_f32
):
    batch, heads_local, head_dim = queries.shape
    kv_local, rows = keys.shape[1], keys.shape[2]
    group = heads_local // kv_local
    block = lax.axis_index("seq")
    keys_out[...] = keys[...]
    values_out[...] = values[...]
    for b in range(batch):

        @pl.when(new_block[b] == block)
        def _():
            start = pl.multiple_of((fill[b] // 16) * 16, 16)
            hit = lax.broadcasted_iota(jnp.int32, (16, head_dim), 0) == fill[b] - start
            for k in range(kv_local):
                for new, out in ((new_keys, keys_out), (new_values, values_out)):
                    old = out[b, k, pl.ds(start, 16), :].astype(F32)
                    row = new[b, k : k + 1, :].astype(F32)
                    out[b, k, pl.ds(start, 16), :] = jnp.where(hit, row, old).astype(BF16)

    lane = lax.broadcasted_iota(jnp.int32, (group, rows), 1)
    for b in range(batch):
        target = jnp.where(new_block[b] == block, fill[b], -1)
        live = (lane < fill[b]) | (lane == target)
        for k in range(kv_local):
            query = queries[b, k * group : (k + 1) * group, :]
            scores = nt_dot(query, keys_out[b, k]) * head_dim ** (-0.5)
            scores = jnp.where(live, scores, -1e30)
            top = jnp.max(scores, axis=1, keepdims=True).astype(BF16).astype(F32)
            weights = jnp.where(live, jnp.exp(scores - top), 0.0).astype(BF16)
            total = jnp.sum(weights.astype(F32), axis=1, keepdims=True)
            summed = jnp.dot(weights, values_out[b, k], preferred_element_type=F32)
            high = total.astype(BF16).astype(F32)
            stats = jnp.where(lane < 32, top, jnp.where(lane < 64, high, total - high))
            base = k * group * 16 + b
            rows_f32[pl.ds(base, group, stride=16), :] = summed
            rows_f32[pl.ds(base + 8, group, stride=16), :] = stats
    payload[...] = rows_f32[...].reshape(heads_local, 16, head_dim).astype(BF16)


def combine_kernel(parts, out):
    sources = parts.shape[0]
    tiles = [parts[s].astype(F32) for s in range(sources)]
    stats = [t[8:16] for t in tiles]
    top = functools.reduce(jnp.maximum, stats)
    weights = [jnp.exp(jnp.minimum(s - top, 0.0)) for s in stats]
    total = 0.0
    for s, w in zip(stats, weights):
        total = total + w * (pltpu.roll(s, 96, 1) + pltpu.roll(s, 64, 1))
    scale = 1.0 / total
    heads = 0.0
    for t, w in zip(tiles, weights):
        heads = heads + t[0:8] * (w * scale)[:, 0:1]
    heads = heads.astype(BF16)
    for p in range(out.shape[0]):
        out[p] = heads


def lanes(tiles, first, count):
    return jnp.concatenate([tiles[first + i] for i in range(count)], axis=1)


def project_kernel(heads, residual, gain, weight, mixed_out, payload, buffer, sems):
    depth = weight.shape[0]
    chunks = depth // CHUNK
    per = CHUNK // 128
    copies = []
    for c in range(chunks):
        part = pl.ds(c * CHUNK, CHUNK)
        copy = pltpu.make_async_copy(weight.at[part, :], buffer.at[part, :], sems.at[c])
        copy.start()
        copies.append(copy)
    total = residual[...]
    for c in range(chunks):
        copies[c].wait()
        total = total + jnp.dot(
            lanes(heads, c * per, per), buffer[pl.ds(c * CHUNK, CHUNK), :], preferred_element_type=F32
        )
    mixed_out[...] = total
    square = jnp.sum(total * total, axis=1, keepdims=True)
    high = square.astype(BF16).astype(F32)
    lane = lax.broadcasted_iota(jnp.int32, total.shape, 1)
    stats = jnp.where(lane < 64, high, square - high)
    tile = jnp.concatenate([total * gain[...], stats], axis=0).astype(BF16)
    for p in range(payload.shape[0]):
        payload[p] = tile


def feed_kernel(tiles, gate, up, down, out, gate_buf, up_buf, down_buf, sems):
    features = gate.shape[1]
    chunks = features // CHUNK
    per = CHUNK // 128
    copies = {}
    for c in range(chunks):
        part = pl.ds(c * CHUNK, CHUNK)
        for kind, (source, target) in enumerate(((gate, gate_buf), (up, up_buf))):
            copies[kind, c] = pltpu.make_async_copy(source.at[:, part], target.at[c], sems.at[kind, c])
            copies[kind, c].start()
    for c in range(chunks):
        copies[2, c] = pltpu.make_async_copy(down.at[:, pl.ds(c * CHUNK, CHUNK)], down_buf.at[c], sems.at[2, c])
        copies[2, c].start()
    squares = 0.0
    for p in range(tiles.shape[0]):
        squares = squares + tiles[p].astype(F32)
    squares = squares[8:16]
    squares = squares + pltpu.roll(squares, 64, 1)
    factor = lax.rsqrt(squares[:, 0:1] / features + 1e-05)
    gate_sum = 0.0
    up_sum = 0.0
    for c in range(chunks):
        piece = lanes(tiles, c * per, per)
        copies[0, c].wait()
        gate_sum = gate_sum + nt_dot(piece, gate_buf[c])
        copies[1, c].wait()
        up_sum = up_sum + nt_dot(piece, up_buf[c])
    gate_sum = gate_sum[0:8] * factor
    up_sum = up_sum[0:8] * factor
    hidden = (gate_sum / (1.0 + jnp.exp(-gate_sum)) * up_sum).astype(BF16)
    for c in range(chunks):
        copies[2, c].wait()
        sums = jnp.dot(hidden, down_buf[c], preferred_element_type=F32).astype(BF16)
        for i in range(per):
            out[c * per + i] = sums[:, i * 128 : (i + 1) * 128]


def finish_kernel(sums, mixed, out):
    total = mixed[...]
    for p in range(sums.shape[0]):
        total = total + sums[p].astype(F32)
    out[...] = total.astype(BF16)


def body(
    queries,
    key_cache,
    value_cache,
    new_keys,
    new_values,
    block_fill,
    new_block,
    residual,
    norm_gain,
    out_weight,
    gate_weight,
    up_weight,
    down_weight,
):
    batch, heads_local, head_dim = queries.shape
    devices = lax.axis_size("kvh") * lax.axis_size("seq")
    hidden, features = gate_weight.shape
    chunks = features // CHUNK
    columns = residual.shape[1]

    keys_out, values_out, partials = pl.pallas_call(
        attention_kernel,
        out_shape=(
            jax.ShapeDtypeStruct(key_cache.shape, BF16),
            jax.ShapeDtypeStruct(value_cache.shape, BF16),
            jax.ShapeDtypeStruct((heads_local, 16, head_dim), BF16),
        ),
        in_specs=[SMEM, SMEM] + [VMEM] * 5,
        out_specs=(VMEM, VMEM, VMEM),
        scratch_shapes=[pltpu.VMEM((heads_local * 16, head_dim), F32)],
        compiler_params=pltpu.CompilerParams(vmem_limit_bytes=8 * MIB),
        name="attention",
    )(new_block, block_fill.reshape(batch), queries, key_cache, value_cache, new_keys, new_values)
    partials = lax.all_to_all(partials, "seq", 0, 0)

    heads = pl.pallas_call(
        combine_kernel,
        out_shape=jax.ShapeDtypeStruct((devices, batch, head_dim), BF16),
        in_specs=[VMEM],
        out_specs=VMEM,
        compiler_params=pltpu.CompilerParams(vmem_limit_bytes=4 * MIB),
        name="combine",
    )(partials)
    heads = lax.all_to_all(heads, EVERY, 0, 0)

    mixed, stream = pl.pallas_call(
        project_kernel,
        out_shape=(
            jax.ShapeDtypeStruct((batch, columns), F32),
            jax.ShapeDtypeStruct((devices, 2 * batch, columns), BF16),
        ),
        in_specs=[VMEM, VMEM, VMEM, ANY],
        out_specs=(VMEM, VMEM),
        scratch_shapes=[
            pltpu.VMEM(out_weight.shape, BF16),
            pltpu.SemaphoreType.DMA((out_weight.shape[0] // CHUNK,)),
        ],
        compiler_params=pltpu.CompilerParams(vmem_limit_bytes=12 * MIB),
        name="project",
    )(heads, residual, norm_gain.reshape(1, columns), out_weight)
    stream = lax.all_to_all(stream, EVERY, 0, 0)

    sums = pl.pallas_call(
        feed_kernel,
        out_shape=jax.ShapeDtypeStruct((devices, batch, columns), BF16),
        in_specs=[VMEM, ANY, ANY, ANY],
        out_specs=VMEM,
        scratch_shapes=[pltpu.VMEM((chunks, hidden, CHUNK), BF16)] * 3 + [pltpu.SemaphoreType.DMA((3, chunks))],
        compiler_params=pltpu.CompilerParams(vmem_limit_bytes=32 * MIB),
        name="feed",
    )(stream, gate_weight, up_weight, down_weight)
    sums = lax.all_to_all(sums, EVERY, 0, 0)

    layer_out = pl.pallas_call(
        finish_kernel,
        out_shape=jax.ShapeDtypeStruct((batch, columns), BF16),
        in_specs=[VMEM, VMEM],
        out_specs=VMEM,
        compiler_params=pltpu.CompilerParams(vmem_limit_bytes=4 * MIB),
        name="finish",
    )(sums, mixed)
    return (layer_out, keys_out, values_out)


def solution(mesh):
    placed = (
        P(None, "kvh", None),
        P(None, "kvh", "seq", None),
        P(None, "kvh", "seq", None),
        P(None, "kvh", None),
        P(None, "kvh", None),
        P(None, "seq"),
        P(),
        P(None, ("kvh", "seq")),
        P(("kvh", "seq")),
        P(None, ("kvh", "seq")),
        P(("kvh", "seq"), None),
        P(("kvh", "seq"), None),
        P(("kvh", "seq"), None),
    )
    return jax.shard_map(
        body,
        mesh=mesh,
        in_specs=placed,
        out_specs=(
            P(None, ("kvh", "seq")),
            P(None, "kvh", "seq", None),
            P(None, "kvh", "seq", None),
        ),
        check_vma=False,
    )
```

```python
import functools

import jax
import jax.numpy as jnp
from jax import lax
from jax.experimental import pallas as pl
from jax.experimental.pallas import tpu as pltpu
from jax.sharding import PartitionSpec as P

F32 = jnp.float32
BF16 = jnp.bfloat16
EVERY = ("kvh", "seq")
VMEM = pl.BlockSpec(memory_space=pltpu.VMEM)
ANY = pl.BlockSpec(memory_space=pl.ANY)
MIB = 1 << 20
CHUNK = 2048
COST = pl.CostEstimate(flops=20 * 10**9, bytes_accessed=60 * 10**6, transcendentals=20 * 10**6)


def nt_dot(a, b):
    return lax.dot_general(a, b, (((1,), (1,)), ((), ())), preferred_element_type=F32)


def tree_sum(terms):
    terms = list(terms)
    while len(terms) > 1:
        paired = [a + b for a, b in zip(terms[0::2], terms[1::2])]
        terms = paired + terms[len(paired) * 2 :]
    return terms[0]


def start_copies(pairs, sems, first=0):
    copies = [pltpu.make_async_copy(src, dst, sems.at[first + i]) for i, (src, dst) in enumerate(pairs)]
    for copy in copies:
        copy.start()
    return copies


def wait_copies(copies):
    for copy in copies:
        copy.wait()


def place_rows(block, new_block, fill, caches):
    batch, kv_local, _, head_dim = caches[0][1].shape
    for b in range(batch):

        @pl.when(new_block[b] == block)
        def _():
            start = pl.multiple_of((fill[b] // 16) * 16, 16)
            hit = lax.broadcasted_iota(jnp.int32, (16, head_dim), 0) == fill[b] - start
            for k in range(kv_local):
                for new, cache in caches:
                    old = cache[b, k, pl.ds(start, 16), :].astype(F32)
                    row = new[b, k : k + 1, :].astype(F32)
                    cache[b, k, pl.ds(start, 16), :] = jnp.where(hit, row, old).astype(BF16)


def attention_kernel(
    new_block_hbm,
    fill_hbm,
    queries_hbm,
    keys_hbm,
    values_hbm,
    new_keys_hbm,
    new_values_hbm,
    payload,
    keys_out,
    values_out,
    new_block,
    fill,
    queries,
    keys,
    values,
    new_keys,
    new_values,
    rows_f32,
    sems,
):
    batch, heads_local, head_dim = queries.shape
    kv_local, rows = keys.shape[1], keys.shape[2]
    group = heads_local // kv_local
    block = lax.axis_index("seq")
    copies = start_copies(
        (
            (keys_hbm, keys),
            (values_hbm, values),
            (queries_hbm, queries),
            (new_keys_hbm, new_keys),
            (new_values_hbm, new_values),
            (new_block_hbm, new_block),
            (fill_hbm, fill),
        ),
        sems,
    )
    wait_copies(copies)
    place_rows(block, new_block, fill, ((new_keys, keys), (new_values, values)))
    writes = start_copies(((keys, keys_out), (values, values_out)), sems, len(copies))

    lane = lax.broadcasted_iota(jnp.int32, (group, rows), 1)
    places = [(b, k) for b in range(batch) for k in range(kv_local)]
    live = [lane < fill[b] + jnp.where(new_block[b] == block, 1, 0) for b in range(batch)]
    scores = [nt_dot(queries[b, k * group : (k + 1) * group, :], keys[b, k]) for b, k in places]
    scores = [jnp.where(live[b], s * head_dim ** (-0.5), -1e30) for (b, _), s in zip(places, scores)]
    tops = [jnp.max(s, axis=1, keepdims=True).astype(BF16).astype(F32) for s in scores]
    weights = [
        jnp.where(live[b], jnp.exp(s - t), 0.0).astype(BF16) for (b, _), s, t in zip(places, scores, tops)
    ]
    sums = [jnp.dot(w, values[b, k], preferred_element_type=F32) for (b, k), w in zip(places, weights)]
    totals = [jnp.sum(w.astype(F32), axis=1, keepdims=True) for w in weights]
    for (b, k), top, total, summed in zip(places, tops, totals, sums):
        high = total.astype(BF16).astype(F32)
        stats = jnp.where(lane < 32, top, jnp.where(lane < 64, high, total - high))
        base = k * group * 16 + b
        rows_f32[pl.ds(base, group, stride=16), :] = summed
        rows_f32[pl.ds(base + 8, group, stride=16), :] = stats
    payload[...] = rows_f32[...].reshape(heads_local, 16, head_dim).astype(BF16)
    wait_copies(writes)


def combine_kernel(parts, out):
    sources = parts.shape[0]
    tiles = [parts[s].astype(F32) for s in range(sources)]
    stats = [t[8:16] for t in tiles]
    top = functools.reduce(jnp.maximum, stats)
    weights = [jnp.exp(jnp.minimum(s - top, 0.0)) for s in stats]
    total = tree_sum(w * (pltpu.roll(s, 96, 1) + pltpu.roll(s, 64, 1)) for s, w in zip(stats, weights))
    scale = 1.0 / total
    heads = tree_sum(t[0:8] * (w * scale)[:, 0:1] for t, w in zip(tiles, weights)).astype(BF16)
    for p in range(out.shape[0]):
        out[p] = heads


def project_kernel(heads, residual, gain, weight, mixed_out, payload):
    per = CHUNK // 128
    total = residual[...] + tree_sum(
        jnp.dot(
            jnp.concatenate([heads[c * per + i] for i in range(per)], axis=1),
            weight[c * CHUNK : (c + 1) * CHUNK, :],
            preferred_element_type=F32,
        )
        for c in range(weight.shape[0] // CHUNK)
    )
    mixed_out[...] = total
    square = jnp.sum(total * total, axis=1, keepdims=True)
    high = square.astype(BF16).astype(F32)
    low = square - high
    lane = lax.broadcasted_iota(jnp.int32, (2, total.shape[1]), 1)
    stats = jnp.zeros(lane.shape, F32)
    for b in range(total.shape[0]):
        stats = jnp.where(lane == b, high[b : b + 1], jnp.where(lane == 64 + b, low[b : b + 1], stats))
    tile = jnp.concatenate([total * gain[...], stats], axis=0).astype(BF16)
    for j in range(payload.shape[1]):
        pair = tile[2 * j : 2 * j + 2]
        for p in range(payload.shape[0]):
            payload[p, j] = pair


def feed_kernel(tiles, gate, up, down, out):
    features = gate.shape[1]
    chunks = features // CHUNK
    per = CHUNK // 128
    squares = tree_sum(tiles[p, 4].astype(F32) for p in range(tiles.shape[0]))
    squares = squares + pltpu.roll(squares, 64, 1)
    factor = jnp.concatenate([lax.rsqrt(squares[0:1, b : b + 1] / features + 1e-05) for b in range(8)], axis=0)
    gate_sum = 0.0
    up_sum = 0.0
    for c in range(chunks):
        piece = jnp.concatenate(
            [jnp.concatenate([tiles[c * per + i, j] for j in range(4)], axis=0) for i in range(per)], axis=1
        )
        part = slice(c * CHUNK, (c + 1) * CHUNK)
        gate_sum = gate_sum + nt_dot(gate[:, part], piece)
        up_sum = up_sum + nt_dot(up[:, part], piece)
    gate_sum = gate_sum.T * factor
    up_sum = up_sum.T * factor
    hidden = (gate_sum / (1.0 + jnp.exp(-gate_sum)) * up_sum).astype(BF16)
    for c in range(chunks):
        sums = jnp.dot(hidden, down[:, c * CHUNK : (c + 1) * CHUNK], preferred_element_type=F32).astype(BF16)
        for i in range(per):
            out[c * per + i] = sums[:, i * 128 : (i + 1) * 128]


def finish_kernel(sums, mixed, out):
    total = tree_sum(sums[p].astype(F32) for p in range(sums.shape[0]))
    out[...] = (mixed[...] + total).astype(BF16)


def in_hbm(x):
    return pltpu.with_memory_space_constraint(x, pltpu.HBM)


def call(kernel, name, operands, in_specs, out_shape, out_specs, scratch=()):
    return pl.pallas_call(
        kernel,
        out_shape=out_shape,
        in_specs=in_specs,
        out_specs=out_specs,
        scratch_shapes=list(scratch),
        compiler_params=pltpu.CompilerParams(vmem_limit_bytes=4 * MIB),
        cost_estimate=COST,
        name=name,
    )(*operands)


def body(
    queries,
    key_cache,
    value_cache,
    new_keys,
    new_values,
    block_fill,
    new_block,
    residual,
    norm_gain,
    out_weight,
    gate_weight,
    up_weight,
    down_weight,
):
    batch, heads_local, head_dim = queries.shape
    devices = lax.axis_size("kvh") * lax.axis_size("seq")
    columns = residual.shape[1]
    fill = block_fill.reshape(batch)
    counts = [pltpu.SMEM((batch,), jnp.int32)] * 2
    caches = [pltpu.VMEM(key_cache.shape, BF16)] * 2
    fresh = [pltpu.VMEM(new_keys.shape, BF16)] * 2

    partials, keys_out, values_out = call(
        attention_kernel,
        "attention",
        [*map(in_hbm, (new_block, fill, queries, key_cache, value_cache, new_keys, new_values))],
        [ANY] * 7,
        (
            jax.ShapeDtypeStruct((heads_local, 16, head_dim), BF16),
            jax.ShapeDtypeStruct(key_cache.shape, BF16),
            jax.ShapeDtypeStruct(value_cache.shape, BF16),
        ),
        (VMEM, ANY, ANY),
        [
            *counts,
            pltpu.VMEM(queries.shape, BF16),
            *caches,
            *fresh,
            pltpu.VMEM((heads_local * 16, head_dim), F32),
            pltpu.SemaphoreType.DMA((9,)),
        ],
    )
    gathered = lax.all_to_all(partials, "seq", 0, 0)
    heads = call(
        combine_kernel,
        "combine",
        [gathered],
        [VMEM],
        jax.ShapeDtypeStruct((devices, batch, head_dim), BF16),
        VMEM,
    )
    all_heads = lax.all_to_all(heads, EVERY, 0, 0)
    mixed, stream = call(
        project_kernel,
        "project",
        [all_heads, residual, norm_gain.reshape(1, columns), out_weight],
        [VMEM] * 4,
        (
            jax.ShapeDtypeStruct((batch, columns), F32),
            jax.ShapeDtypeStruct((devices, batch // 2 + 1, 2, columns), BF16),
        ),
        (VMEM, VMEM),
    )
    all_stream = lax.all_to_all(stream, EVERY, 0, 0)
    sums = call(
        feed_kernel,
        "feed",
        [all_stream, gate_weight, up_weight, down_weight],
        [VMEM] * 4,
        jax.ShapeDtypeStruct((devices, batch, columns), BF16),
        VMEM,
    )
    all_sums = lax.all_to_all(sums, EVERY, 0, 0)
    layer_out = call(
        finish_kernel,
        "finish",
        [all_sums, mixed],
        [VMEM] * 2,
        jax.ShapeDtypeStruct((batch, columns), BF16),
        VMEM,
    )
    return (layer_out, keys_out, values_out)


def solution(mesh):
    placed = (
        P(None, "kvh", None),
        P(None, "kvh", "seq", None),
        P(None, "kvh", "seq", None),
        P(None, "kvh", None),
        P(None, "kvh", None),
        P(None, "seq"),
        P(),
        P(None, ("kvh", "seq")),
        P(("kvh", "seq")),
        P(None, ("kvh", "seq")),
        P(("kvh", "seq"), None),
        P(("kvh", "seq"), None),
        P(("kvh", "seq"), None),
    )
    return jax.shard_map(
        body,
        mesh=mesh,
        in_specs=placed,
        out_specs=(
            P(None, ("kvh", "seq")),
            P(None, "kvh", "seq", None),
            P(None, "kvh", "seq", None),
        ),
        check_vma=False,
    )
```

```python
import functools

import jax
import jax.numpy as jnp
from jax import lax
from jax.experimental import pallas as pl
from jax.experimental.pallas import tpu as pltpu
from jax.sharding import PartitionSpec as P

F32 = jnp.float32
BF16 = jnp.bfloat16
EVERY = ("kvh", "seq")
VMEM = pl.BlockSpec(memory_space=pltpu.VMEM)
ANY = pl.BlockSpec(memory_space=pl.ANY)
MIB = 1 << 20
CHUNK = 2048
STEP = 256
COST = pl.CostEstimate(flops=20 * 10**9, bytes_accessed=60 * 10**6, transcendentals=20 * 10**6)


def nt_dot(a, b):
    return lax.dot_general(a, b, (((1,), (1,)), ((), ())), preferred_element_type=F32)


def tree_sum(terms):
    terms = list(terms)
    while len(terms) > 1:
        paired = [a + b for a, b in zip(terms[0::2], terms[1::2])]
        terms = paired + terms[len(paired) * 2 :]
    return terms[0]


def start_copies(pairs, sems, first=0):
    copies = [pltpu.make_async_copy(src, dst, sems.at[first + i]) for i, (src, dst) in enumerate(pairs)]
    for copy in copies:
        copy.start()
    return copies


def wait_copies(copies):
    for copy in copies:
        copy.wait()


def place_rows(block, new_block, fill, caches):
    batch, kv_local, _, head_dim = caches[0][1].shape
    for b in range(batch):

        @pl.when(new_block[b] == block)
        def _():
            start = pl.multiple_of((fill[b] // 16) * 16, 16)
            hit = lax.broadcasted_iota(jnp.int32, (16, head_dim), 0) == fill[b] - start
            for k in range(kv_local):
                for new, cache in caches:
                    old = cache[b, k, pl.ds(start, 16), :].astype(F32)
                    row = new[b, k : k + 1, :].astype(F32)
                    cache[b, k, pl.ds(start, 16), :] = jnp.where(hit, row, old).astype(BF16)


def attention_kernel(
    new_block_hbm,
    fill_hbm,
    queries_hbm,
    keys_hbm,
    values_hbm,
    new_keys_hbm,
    new_values_hbm,
    payload,
    keys,
    values,
    new_block,
    fill,
    queries,
    new_keys,
    new_values,
    rows_f32,
    sems,
):
    batch, heads_local, head_dim = queries.shape
    kv_local, rows = keys.shape[1], keys.shape[2]
    group = heads_local // kv_local
    block = lax.axis_index("seq")
    copies = start_copies(
        (
            (keys_hbm, keys),
            (values_hbm, values),
            (queries_hbm, queries),
            (new_keys_hbm, new_keys),
            (new_values_hbm, new_values),
            (new_block_hbm, new_block),
            (fill_hbm, fill),
        ),
        sems,
    )
    wait_copies(copies)
    place_rows(block, new_block, fill, ((new_keys, keys), (new_values, values)))

    lane = lax.broadcasted_iota(jnp.int32, (group, rows), 1)
    places = [(b, k) for b in range(batch) for k in range(kv_local)]
    live = [lane < fill[b] + jnp.where(new_block[b] == block, 1, 0) for b in range(batch)]
    scores = [nt_dot(queries[b, k * group : (k + 1) * group, :], keys[b, k]) for b, k in places]
    scores = [jnp.where(live[b], s * head_dim ** (-0.5), -1e30) for (b, _), s in zip(places, scores)]
    tops = [jnp.max(s, axis=1, keepdims=True).astype(BF16).astype(F32) for s in scores]
    weights = [
        jnp.where(live[b], jnp.exp(s - t), 0.0).astype(BF16) for (b, _), s, t in zip(places, scores, tops)
    ]
    sums = [jnp.dot(w, values[b, k], preferred_element_type=F32) for (b, k), w in zip(places, weights)]
    totals = [jnp.sum(w.astype(F32), axis=1, keepdims=True) for w in weights]
    for (b, k), top, total, summed in zip(places, tops, totals, sums):
        high = total.astype(BF16).astype(F32)
        stats = jnp.where(lane < 32, top, jnp.where(lane < 64, high, total - high))
        base = k * group * 16 + b
        rows_f32[pl.ds(base, group, stride=16), :] = summed
        rows_f32[pl.ds(base + 8, group, stride=16), :] = stats
    payload[...] = rows_f32[...].reshape(heads_local, 16, head_dim).astype(BF16)


def combine_kernel(parts, out):
    sources = parts.shape[0]
    tiles = [parts[s].astype(F32) for s in range(sources)]
    stats = [t[8:16] for t in tiles]
    top = functools.reduce(jnp.maximum, stats)
    weights = [jnp.exp(jnp.minimum(s - top, 0.0)) for s in stats]
    total = tree_sum(w * (pltpu.roll(s, 96, 1) + pltpu.roll(s, 64, 1)) for s, w in zip(stats, weights))
    scale = 1.0 / total
    heads = tree_sum(t[0:8] * (w * scale)[:, 0:1] for t, w in zip(tiles, weights)).astype(BF16)
    for p in range(out.shape[0]):
        out[p] = heads


def project_kernel(heads, residual, gain, weight, mixed_out, payload):
    per = CHUNK // 128
    total = residual[...] + tree_sum(
        jnp.dot(
            jnp.concatenate([heads[c * per + i] for i in range(per)], axis=1),
            weight[c * CHUNK : (c + 1) * CHUNK, :],
            preferred_element_type=F32,
        )
        for c in range(weight.shape[0] // CHUNK)
    )
    mixed_out[...] = total
    square = jnp.sum(total * total, axis=1, keepdims=True)
    high = square.astype(BF16).astype(F32)
    low = square - high
    lane = lax.broadcasted_iota(jnp.int32, (2, total.shape[1]), 1)
    stats = jnp.zeros(lane.shape, F32)
    for b in range(total.shape[0]):
        stats = jnp.where(lane == b, high[b : b + 1], jnp.where(lane == 64 + b, low[b : b + 1], stats))
    tile = jnp.concatenate([total * gain[...], stats], axis=0).astype(BF16)
    for j in range(payload.shape[1]):
        pair = tile[2 * j : 2 * j + 2]
        for p in range(payload.shape[0]):
            payload[p, j] = pair


def feed_kernel(tiles, gate, up, down, keys, values, out, keys_out, values_out, sems):
    writes = start_copies(((keys, keys_out), (values, values_out)), sems)
    features = gate.shape[1]
    squares = tree_sum(tiles[p, 4].astype(F32) for p in range(tiles.shape[0]))
    squares = squares + pltpu.roll(squares, 64, 1)
    factor = jnp.concatenate([lax.rsqrt(squares[0:1, b : b + 1] / features + 1e-05) for b in range(8)], axis=0)
    gate_sum = 0.0
    up_sum = 0.0
    for c in range(features // STEP):
        first = c * STEP // 128
        piece = jnp.concatenate(
            [
                jnp.concatenate([tiles[first + i, j] for j in range(tiles.shape[1] - 1)], axis=0)
                for i in range(STEP // 128)
            ],
            axis=1,
        )
        part = slice(c * STEP, (c + 1) * STEP)
        gate_sum = gate_sum + nt_dot(gate[:, part], piece)
        up_sum = up_sum + nt_dot(piece, up[:, part])
    gate_sum = gate_sum.T * factor
    up_sum = up_sum * factor
    hidden = (gate_sum / (1.0 + jnp.exp(-gate_sum)) * up_sum).astype(BF16)
    per = CHUNK // 128
    for c in range(features // CHUNK):
        sums = jnp.dot(hidden, down[:, c * CHUNK : (c + 1) * CHUNK], preferred_element_type=F32).astype(BF16)
        for i in range(per):
            out[c * per + i] = sums[:, i * 128 : (i + 1) * 128]
    wait_copies(writes)


def finish_kernel(sums, mixed, out):
    total = tree_sum(sums[p].astype(F32) for p in range(sums.shape[0]))
    out[...] = (mixed[...] + total).astype(BF16)


def in_hbm(x):
    return pltpu.with_memory_space_constraint(x, pltpu.HBM)


def call(kernel, name, operands, in_specs, out_shape, out_specs, scratch=()):
    return pl.pallas_call(
        kernel,
        out_shape=out_shape,
        in_specs=in_specs,
        out_specs=out_specs,
        scratch_shapes=list(scratch),
        compiler_params=pltpu.CompilerParams(vmem_limit_bytes=4 * MIB),
        cost_estimate=COST,
        name=name,
    )(*operands)


def body(
    queries,
    key_cache,
    value_cache,
    new_keys,
    new_values,
    block_fill,
    new_block,
    residual,
    norm_gain,
    out_weight,
    gate_weight,
    up_weight,
    down_weight,
):
    batch, heads_local, head_dim = queries.shape
    devices = lax.axis_size("kvh") * lax.axis_size("seq")
    columns = residual.shape[1]
    fill = block_fill.reshape(batch)
    counts = [pltpu.SMEM((batch,), jnp.int32)] * 2
    fresh = [pltpu.VMEM(new_keys.shape, BF16)] * 2

    partials, held_keys, held_values = call(
        attention_kernel,
        "attention",
        [*map(in_hbm, (new_block, fill, queries, key_cache, value_cache, new_keys, new_values))],
        [ANY] * 7,
        (
            jax.ShapeDtypeStruct((heads_local, 16, head_dim), BF16),
            pltpu.VMEM(key_cache.shape, BF16),
            pltpu.VMEM(value_cache.shape, BF16),
        ),
        (VMEM, VMEM, VMEM),
        [
            *counts,
            pltpu.VMEM(queries.shape, BF16),
            *fresh,
            pltpu.VMEM((heads_local * 16, head_dim), F32),
            pltpu.SemaphoreType.DMA((7,)),
        ],
    )
    gathered = lax.all_to_all(partials, "seq", 0, 0)
    heads = call(
        combine_kernel,
        "combine",
        [gathered],
        [VMEM],
        jax.ShapeDtypeStruct((devices, batch, head_dim), BF16),
        VMEM,
    )
    all_heads = lax.all_to_all(heads, EVERY, 0, 0)
    mixed, stream = call(
        project_kernel,
        "project",
        [all_heads, residual, norm_gain.reshape(1, columns), out_weight],
        [VMEM] * 4,
        (
            jax.ShapeDtypeStruct((batch, columns), F32),
            jax.ShapeDtypeStruct((devices, batch // 2 + 1, 2, columns), BF16),
        ),
        (VMEM, VMEM),
    )
    all_stream = lax.all_to_all(stream, EVERY, 0, 0)
    sums, keys_out, values_out = call(
        feed_kernel,
        "feed",
        [all_stream, gate_weight, up_weight, down_weight, held_keys, held_values],
        [VMEM] * 6,
        (
            jax.ShapeDtypeStruct((devices, batch, columns), BF16),
            jax.ShapeDtypeStruct(key_cache.shape, BF16),
            jax.ShapeDtypeStruct(value_cache.shape, BF16),
        ),
        (VMEM, ANY, ANY),
        [pltpu.SemaphoreType.DMA((2,))],
    )
    all_sums = lax.all_to_all(sums, EVERY, 0, 0)
    layer_out = call(
        finish_kernel,
        "finish",
        [all_sums, mixed],
        [VMEM] * 2,
        jax.ShapeDtypeStruct((batch, columns), BF16),
        VMEM,
    )
    return (layer_out, keys_out, values_out)


def solution(mesh):
    placed = (
        P(None, "kvh", None),
        P(None, "kvh", "seq", None),
        P(None, "kvh", "seq", None),
        P(None, "kvh", None),
        P(None, "kvh", None),
        P(None, "seq"),
        P(),
        P(None, ("kvh", "seq")),
        P(("kvh", "seq")),
        P(None, ("kvh", "seq")),
        P(("kvh", "seq"), None),
        P(("kvh", "seq"), None),
        P(("kvh", "seq"), None),
    )
    return jax.shard_map(
        body,
        mesh=mesh,
        in_specs=placed,
        out_specs=(
            P(None, ("kvh", "seq")),
            P(None, "kvh", "seq", None),
            P(None, "kvh", "seq", None),
        ),
        check_vma=False,
    )
```

```python
import functools

import jax
import jax.numpy as jnp
from jax import lax
from jax.experimental import pallas as pl
from jax.experimental.pallas import tpu as pltpu
from jax.sharding import PartitionSpec as P

F32 = jnp.float32
BF16 = jnp.bfloat16
EVERY = ("kvh", "seq")
VMEM = pl.BlockSpec(memory_space=pltpu.VMEM)
ANY = pl.BlockSpec(memory_space=pl.ANY)
MIB = 1 << 20
CHUNK = 2048
STEP = 256
COST = pl.CostEstimate(flops=20 * 10**9, bytes_accessed=60 * 10**6, transcendentals=20 * 10**6)


def nt_dot(a, b):
    return lax.dot_general(a, b, (((1,), (1,)), ((), ())), preferred_element_type=F32)


def tree_sum(terms):
    terms = list(terms)
    while len(terms) > 1:
        paired = [a + b for a, b in zip(terms[0::2], terms[1::2])]
        terms = paired + terms[len(paired) * 2 :]
    return terms[0]


def start_copies(pairs, sems, first=0):
    copies = [pltpu.make_async_copy(src, dst, sems.at[first + i]) for i, (src, dst) in enumerate(pairs)]
    for copy in copies:
        copy.start()
    return copies


def wait_copies(copies):
    for copy in copies:
        copy.wait()


def place_row(block, new_block, fill, new, cache):
    batch, kv_local, _, head_dim = cache.shape
    request = jnp.int32(-1)
    for b in range(batch):
        request = jnp.where(new_block[b] == block, b, request)

    @pl.when(request >= 0)
    def _():
        row = fill[request]
        start = pl.multiple_of((row // 16) * 16, 16)
        hit = lax.broadcasted_iota(jnp.int32, (16, head_dim), 0) == row - start
        for k in range(kv_local):
            old = cache[request, k, pl.ds(start, 16), :].astype(F32)
            fresh = new[request, k : k + 1, :].astype(F32)
            cache[request, k, pl.ds(start, 16), :] = jnp.where(hit, fresh, old).astype(BF16)


def attention_kernel(
    new_block_hbm,
    fill_hbm,
    queries_hbm,
    keys_hbm,
    values_hbm,
    new_keys_hbm,
    new_values_hbm,
    payload,
    keys,
    values,
    new_block,
    fill,
    queries,
    new_keys,
    new_values,
    rows_f32,
    sems,
):
    batch, heads_local, head_dim = queries.shape
    kv_local, rows = keys.shape[1], keys.shape[2]
    group = heads_local // kv_local
    block = lax.axis_index("seq")
    copies = start_copies(
        (
            (keys_hbm, keys),
            (queries_hbm, queries),
            (new_keys_hbm, new_keys),
            (new_block_hbm, new_block),
            (fill_hbm, fill),
            (values_hbm, values),
            (new_values_hbm, new_values),
        ),
        sems,
    )
    wait_copies(copies[:5])
    place_row(block, new_block, fill, new_keys, keys)

    lane = lax.broadcasted_iota(jnp.int32, (group, rows), 1)
    places = [(b, k) for b in range(batch) for k in range(kv_local)]
    live = [lane < fill[b] + jnp.where(new_block[b] == block, 1, 0) for b in range(batch)]
    scores = [nt_dot(queries[b, k * group : (k + 1) * group, :], keys[b, k]) for b, k in places]
    scores = [jnp.where(live[b], s * head_dim ** (-0.5), -1e30) for (b, _), s in zip(places, scores)]
    tops = [jnp.max(s, axis=1, keepdims=True).astype(BF16).astype(F32) for s in scores]
    weights = [
        jnp.where(live[b], jnp.exp(s - t), 0.0).astype(BF16) for (b, _), s, t in zip(places, scores, tops)
    ]
    totals = [jnp.sum(w.astype(F32), axis=1, keepdims=True) for w in weights]
    wait_copies(copies[5:])
    place_row(block, new_block, fill, new_values, values)
    sums = [jnp.dot(w, values[b, k], preferred_element_type=F32) for (b, k), w in zip(places, weights)]
    height = batch + 2
    for (b, k), summed in zip(places, sums):
        rows_f32[pl.ds(k * group * height + b, group, stride=height), :] = summed
    for k in range(kv_local):
        first = jnp.zeros(lane.shape, F32)
        second = jnp.zeros(lane.shape, F32)
        for b in range(batch):
            top, total = tops[b * kv_local + k], totals[b * kv_local + k]
            high = total.astype(BF16).astype(F32)
            first = jnp.where(lane == b, top, jnp.where(lane == 64 + b, high, first))
            second = jnp.where(lane == b, total - high, second)
        rows_f32[pl.ds(k * group * height + batch, group, stride=height), :] = first
        rows_f32[pl.ds(k * group * height + batch + 1, group, stride=height), :] = second
    payload[...] = rows_f32[...].astype(BF16)


def combine_kernel(parts, out, rows):
    batch = out.shape[1]
    height = batch + 2
    sources = parts.shape[0] // height
    rows[...] = parts[...].astype(F32)
    first = rows[pl.ds(batch, sources, stride=height), :]
    second = rows[pl.ds(batch + 1, sources, stride=height), :]
    total = pltpu.roll(first, 64, 1) + second
    weights = jnp.exp(jnp.minimum(first - jnp.max(first, axis=0, keepdims=True), 0.0))
    scale = weights / jnp.sum(weights * total, axis=0, keepdims=True)
    heads = jnp.concatenate(
        [
            jnp.sum(rows[pl.ds(b, sources, stride=height), :] * scale[:, b : b + 1], axis=0, keepdims=True)
            for b in range(batch)
        ],
        axis=0,
    ).astype(BF16)
    for p in range(out.shape[0]):
        out[p] = heads


def project_kernel(heads, residual, gain, weight, mixed_out, payload):
    per = CHUNK // 128
    total = residual[...] + tree_sum(
        jnp.dot(
            jnp.concatenate([heads[c * per + i] for i in range(per)], axis=1),
            weight[c * CHUNK : (c + 1) * CHUNK, :],
            preferred_element_type=F32,
        )
        for c in range(weight.shape[0] // CHUNK)
    )
    mixed_out[...] = total
    square = jnp.sum(total * total, axis=1, keepdims=True)
    high = square.astype(BF16).astype(F32)
    low = square - high
    lane = lax.broadcasted_iota(jnp.int32, (2, total.shape[1]), 1)
    stats = jnp.zeros(lane.shape, F32)
    for b in range(total.shape[0]):
        stats = jnp.where(lane == b, high[b : b + 1], jnp.where(lane == 64 + b, low[b : b + 1], stats))
    tile = jnp.concatenate([total * gain[...], stats], axis=0).astype(BF16)
    whole = jnp.concatenate([tile] * (payload.shape[1] // tile.shape[0]), axis=0)
    for p in range(payload.shape[0]):
        payload[p] = whole


def feed_kernel(tiles, gate, up, down, keys, values, out, keys_out, values_out, sems):
    writes = start_copies(((keys, keys_out), (values, values_out)), sems)
    features = gate.shape[1]
    squares = tree_sum(tiles[p, 4].astype(F32) for p in range(tiles.shape[0]))
    squares = squares + pltpu.roll(squares, 64, 1)
    factor = jnp.concatenate([lax.rsqrt(squares[0:1, b : b + 1] / features + 1e-05) for b in range(8)], axis=0)
    gate_sum = 0.0
    up_sum = 0.0
    for c in range(features // STEP):
        first = c * STEP // 128
        piece = jnp.concatenate(
            [
                jnp.concatenate([tiles[first + i, j] for j in range(tiles.shape[1] - 1)], axis=0)
                for i in range(STEP // 128)
            ],
            axis=1,
        )
        part = slice(c * STEP, (c + 1) * STEP)
        gate_sum = gate_sum + nt_dot(gate[:, part], piece)
        up_sum = up_sum + nt_dot(piece, up[:, part])
    gate_sum = gate_sum.T * factor
    up_sum = up_sum * factor
    hidden = (gate_sum / (1.0 + jnp.exp(-gate_sum)) * up_sum).astype(BF16)
    per = CHUNK // 128
    for c in range(features // CHUNK):
        sums = jnp.dot(hidden, down[:, c * CHUNK : (c + 1) * CHUNK], preferred_element_type=F32).astype(BF16)
        for i in range(per):
            out[c * per + i] = sums[:, i * 128 : (i + 1) * 128]
    wait_copies(writes)


def finish_kernel(sums, mixed, out):
    total = tree_sum(sums[p].astype(F32) for p in range(sums.shape[0]))
    out[...] = (mixed[...] + total).astype(BF16)


def in_hbm(x):
    return pltpu.with_memory_space_constraint(x, pltpu.HBM)


def call(kernel, name, operands, in_specs, out_shape, out_specs, scratch=()):
    return pl.pallas_call(
        kernel,
        out_shape=out_shape,
        in_specs=in_specs,
        out_specs=out_specs,
        scratch_shapes=list(scratch),
        compiler_params=pltpu.CompilerParams(vmem_limit_bytes=4 * MIB),
        cost_estimate=COST,
        name=name,
    )(*operands)


def body(
    queries,
    key_cache,
    value_cache,
    new_keys,
    new_values,
    block_fill,
    new_block,
    residual,
    norm_gain,
    out_weight,
    gate_weight,
    up_weight,
    down_weight,
):
    batch, heads_local, head_dim = queries.shape
    devices = lax.axis_size("kvh") * lax.axis_size("seq")
    columns = residual.shape[1]
    fill = block_fill.reshape(batch)
    counts = [pltpu.SMEM((batch,), jnp.int32)] * 2
    fresh = [pltpu.VMEM(new_keys.shape, BF16)] * 2

    partials, held_keys, held_values = call(
        attention_kernel,
        "attention",
        [*map(in_hbm, (new_block, fill, queries, key_cache, value_cache, new_keys, new_values))],
        [ANY] * 7,
        (
            jax.ShapeDtypeStruct((heads_local * (batch + 2), head_dim), BF16),
            pltpu.VMEM(key_cache.shape, BF16),
            pltpu.VMEM(value_cache.shape, BF16),
        ),
        (VMEM, VMEM, VMEM),
        [
            *counts,
            pltpu.VMEM(queries.shape, BF16),
            *fresh,
            pltpu.VMEM((heads_local * (batch + 2), head_dim), F32),
            pltpu.SemaphoreType.DMA((7,)),
        ],
    )
    partials = partials.reshape(heads_local, batch // 2 + 1, 2, head_dim)
    gathered = lax.all_to_all(partials, "seq", 0, 0).reshape(heads_local * (batch + 2), head_dim)
    heads = call(
        combine_kernel,
        "combine",
        [gathered],
        [VMEM],
        jax.ShapeDtypeStruct((devices, batch, head_dim), BF16),
        VMEM,
        [pltpu.VMEM((heads_local * (batch + 2), head_dim), F32)],
    )
    all_heads = lax.all_to_all(heads, EVERY, 0, 0)
    mixed, stream = call(
        project_kernel,
        "project",
        [all_heads, residual, norm_gain.reshape(1, columns), out_weight],
        [VMEM] * 4,
        (
            jax.ShapeDtypeStruct((batch, columns), F32),
            jax.ShapeDtypeStruct((devices // 8, 8 * (batch + 2), columns), BF16),
        ),
        (VMEM, VMEM),
    )
    stream = stream.reshape(devices, batch // 2 + 1, 2, columns)
    all_stream = lax.all_to_all(stream, EVERY, 0, 0)
    sums, keys_out, values_out = call(
        feed_kernel,
        "feed",
        [all_stream, gate_weight, up_weight, down_weight, held_keys, held_values],
        [VMEM] * 6,
        (
            jax.ShapeDtypeStruct((devices, batch, columns), BF16),
            jax.ShapeDtypeStruct(key_cache.shape, BF16),
            jax.ShapeDtypeStruct(value_cache.shape, BF16),
        ),
        (VMEM, ANY, ANY),
        [pltpu.SemaphoreType.DMA((2,))],
    )
    all_sums = lax.all_to_all(sums, EVERY, 0, 0)
    layer_out = call(
        finish_kernel,
        "finish",
        [all_sums, mixed],
        [VMEM] * 2,
        jax.ShapeDtypeStruct((batch, columns), BF16),
        VMEM,
    )
    return (layer_out, keys_out, values_out)


def solution(mesh):
    placed = (
        P(None, "kvh", None),
        P(None, "kvh", "seq", None),
        P(None, "kvh", "seq", None),
        P(None, "kvh", None),
        P(None, "kvh", None),
        P(None, "seq"),
        P(),
        P(None, ("kvh", "seq")),
        P(("kvh", "seq")),
        P(None, ("kvh", "seq")),
        P(("kvh", "seq"), None),
        P(("kvh", "seq"), None),
        P(("kvh", "seq"), None),
    )
    return jax.shard_map(
        body,
        mesh=mesh,
        in_specs=placed,
        out_specs=(
            P(None, ("kvh", "seq")),
            P(None, "kvh", "seq", None),
            P(None, "kvh", "seq", None),
        ),
        check_vma=False,
    )
```

```python
import functools

import jax
import jax.numpy as jnp
import numpy as np
from jax import lax
from jax.experimental import pallas as pl
from jax.experimental.pallas import tpu as pltpu
from jax.sharding import PartitionSpec as P

F32 = jnp.float32
BF16 = jnp.bfloat16
SEQ = ("y", "z", "core")
EVERY = ("kvh", "y", "z", "core")
SIZES = (4, 4, 4, 2)
ORDER = ("core", "z", "y", "kvh")
SLOT = np.arange(128).reshape(SIZES).transpose([EVERY.index(axis) for axis in ORDER]).reshape(-1).argsort().tolist()
VMEM = pl.BlockSpec(memory_space=pltpu.VMEM)
ANY = pl.BlockSpec(memory_space=pl.ANY)
MIB = 1 << 20
CHUNK = 2048
STEP = 256
COST = pl.CostEstimate(flops=20 * 10**9, bytes_accessed=60 * 10**6, transcendentals=20 * 10**6)


def nt_dot(a, b):
    return lax.dot_general(a, b, (((1,), (1,)), ((), ())), preferred_element_type=F32)


def tree_sum(terms):
    terms = list(terms)
    while len(terms) > 1:
        paired = [a + b for a, b in zip(terms[0::2], terms[1::2])]
        terms = paired + terms[len(paired) * 2 :]
    return terms[0]


def start_copies(pairs, sems, first=0):
    copies = [pltpu.make_async_copy(src, dst, sems.at[first + i]) for i, (src, dst) in enumerate(pairs)]
    for copy in copies:
        copy.start()
    return copies


def wait_copies(copies):
    for copy in copies:
        copy.wait()


def place_row(block, new_block, fill, new, cache):
    batch, kv_local, _, head_dim = cache.shape
    request = jnp.int32(-1)
    for b in range(batch):
        request = jnp.where(new_block[b] == block, b, request)

    @pl.when(request >= 0)
    def _():
        row = fill[request]
        start = pl.multiple_of((row // 16) * 16, 16)
        hit = lax.broadcasted_iota(jnp.int32, (16, head_dim), 0) == row - start
        for k in range(kv_local):
            old = cache[request, k, pl.ds(start, 16), :].astype(F32)
            fresh = new[request, k : k + 1, :].astype(F32)
            cache[request, k, pl.ds(start, 16), :] = jnp.where(hit, fresh, old).astype(BF16)


def attention_kernel(
    new_block_hbm,
    fill_hbm,
    queries_hbm,
    keys_hbm,
    values_hbm,
    new_keys_hbm,
    new_values_hbm,
    payload,
    keys,
    values,
    new_block,
    fill,
    queries,
    new_keys,
    new_values,
    rows_f32,
    sems,
):
    batch, heads_local, head_dim = queries.shape
    kv_local, rows = keys.shape[1], keys.shape[2]
    group = heads_local // kv_local
    block = (lax.axis_index("y") * lax.axis_size("z") + lax.axis_index("z")) * 2 + lax.axis_index("core")
    copies = start_copies(
        (
            (keys_hbm, keys),
            (queries_hbm, queries),
            (new_keys_hbm, new_keys),
            (new_block_hbm, new_block),
            (fill_hbm, fill),
            (values_hbm, values),
            (new_values_hbm, new_values),
        ),
        sems,
    )
    wait_copies(copies[:5])
    place_row(block, new_block, fill, new_keys, keys)

    lane = lax.broadcasted_iota(jnp.int32, (group, rows), 1)
    places = [(b, k) for b in range(batch) for k in range(kv_local)]
    live = [lane < fill[b] + jnp.where(new_block[b] == block, 1, 0) for b in range(batch)]
    scores = [nt_dot(queries[b, k * group : (k + 1) * group, :], keys[b, k]) for b, k in places]
    scores = [jnp.where(live[b], s * head_dim ** (-0.5), -1e30) for (b, _), s in zip(places, scores)]
    tops = [jnp.max(s, axis=1, keepdims=True).astype(BF16).astype(F32) for s in scores]
    weights = [
        jnp.where(live[b], jnp.exp(s - t), 0.0).astype(BF16) for (b, _), s, t in zip(places, scores, tops)
    ]
    totals = [jnp.sum(w.astype(F32), axis=1, keepdims=True) for w in weights]
    wait_copies(copies[5:])
    place_row(block, new_block, fill, new_values, values)
    sums = [jnp.dot(w, values[b, k], preferred_element_type=F32) for (b, k), w in zip(places, weights)]
    height = batch + 2
    for (b, k), summed in zip(places, sums):
        rows_f32[pl.ds(k * group * height + b, group, stride=height), :] = summed
    for k in range(kv_local):
        first = jnp.zeros(lane.shape, F32)
        second = jnp.zeros(lane.shape, F32)
        for b in range(batch):
            top, total = tops[b * kv_local + k], totals[b * kv_local + k]
            high = total.astype(BF16).astype(F32)
            first = jnp.where(lane == b, top, jnp.where(lane == 64 + b, high, first))
            second = jnp.where(lane == b, total - high, second)
        rows_f32[pl.ds(k * group * height + batch, group, stride=height), :] = first
        rows_f32[pl.ds(k * group * height + batch + 1, group, stride=height), :] = second
    payload[...] = rows_f32[...].astype(BF16)


def combine_kernel(parts, out, rows):
    batch = out.shape[1]
    height = batch + 2
    sources = parts.shape[0] // height
    rows[...] = parts[...].astype(F32)
    first = rows[pl.ds(batch, sources, stride=height), :]
    second = rows[pl.ds(batch + 1, sources, stride=height), :]
    total = pltpu.roll(first, 64, 1) + second
    weights = jnp.exp(jnp.minimum(first - jnp.max(first, axis=0, keepdims=True), 0.0))
    scale = weights / jnp.sum(weights * total, axis=0, keepdims=True)
    heads = jnp.concatenate(
        [
            jnp.sum(rows[pl.ds(b, sources, stride=height), :] * scale[:, b : b + 1], axis=0, keepdims=True)
            for b in range(batch)
        ],
        axis=0,
    ).astype(BF16)
    for p in range(out.shape[0]):
        out[p] = heads


def project_kernel(heads, residual, gain, weight, mixed_out, payload):
    per = CHUNK // 128
    total = residual[...] + tree_sum(
        jnp.dot(
            jnp.concatenate([heads[SLOT[c * per + i]] for i in range(per)], axis=1),
            weight[c * CHUNK : (c + 1) * CHUNK, :],
            preferred_element_type=F32,
        )
        for c in range(weight.shape[0] // CHUNK)
    )
    mixed_out[...] = total
    square = jnp.sum(total * total, axis=1, keepdims=True)
    high = square.astype(BF16).astype(F32)
    low = square - high
    lane = lax.broadcasted_iota(jnp.int32, (2, total.shape[1]), 1)
    stats = jnp.zeros(lane.shape, F32)
    for b in range(total.shape[0]):
        stats = jnp.where(lane == b, high[b : b + 1], jnp.where(lane == 64 + b, low[b : b + 1], stats))
    tile = jnp.concatenate([total * gain[...], stats], axis=0).astype(BF16)
    whole = jnp.concatenate([tile] * (payload.shape[1] // tile.shape[0]), axis=0)
    for p in range(payload.shape[0]):
        payload[p] = whole


def feed_kernel(tiles, gate, up, down, keys, values, out, keys_out, values_out, sems):
    writes = start_copies(((keys, keys_out), (values, values_out)), sems)
    features = gate.shape[1]
    squares = tree_sum(tiles[p, 4].astype(F32) for p in range(tiles.shape[0]))
    squares = squares + pltpu.roll(squares, 64, 1)
    factor = jnp.concatenate([lax.rsqrt(squares[0:1, b : b + 1] / features + 1e-05) for b in range(8)], axis=0)
    gate_sum = 0.0
    up_sum = 0.0
    for c in range(features // STEP):
        first = c * STEP // 128
        piece = jnp.concatenate(
            [
                jnp.concatenate([tiles[SLOT[first + i], j] for j in range(tiles.shape[1] - 1)], axis=0)
                for i in range(STEP // 128)
            ],
            axis=1,
        )
        part = slice(c * STEP, (c + 1) * STEP)
        gate_sum = gate_sum + nt_dot(gate[:, part], piece)
        up_sum = up_sum + nt_dot(piece, up[:, part])
    gate_sum = gate_sum.T * factor
    up_sum = up_sum * factor
    hidden = (gate_sum / (1.0 + jnp.exp(-gate_sum)) * up_sum).astype(BF16)
    per = CHUNK // 128
    for c in range(features // CHUNK):
        sums = jnp.dot(hidden, down[:, c * CHUNK : (c + 1) * CHUNK], preferred_element_type=F32).astype(BF16)
        for i in range(per):
            out[SLOT[c * per + i]] = sums[:, i * 128 : (i + 1) * 128]
    wait_copies(writes)


def finish_kernel(sums, mixed, out):
    total = tree_sum(sums[p].astype(F32) for p in range(sums.shape[0]))
    out[...] = (mixed[...] + total).astype(BF16)


def in_hbm(x):
    return pltpu.with_memory_space_constraint(x, pltpu.HBM)


def call(kernel, name, operands, in_specs, out_shape, out_specs, scratch=()):
    return pl.pallas_call(
        kernel,
        out_shape=out_shape,
        in_specs=in_specs,
        out_specs=out_specs,
        scratch_shapes=list(scratch),
        compiler_params=pltpu.CompilerParams(vmem_limit_bytes=4 * MIB),
        cost_estimate=COST,
        name=name,
    )(*operands)


def body(
    queries,
    key_cache,
    value_cache,
    new_keys,
    new_values,
    block_fill,
    new_block,
    residual,
    norm_gain,
    out_weight,
    gate_weight,
    up_weight,
    down_weight,
):
    batch, heads_local, head_dim = queries.shape
    devices = lax.axis_size(EVERY)
    columns = residual.shape[1]
    fill = block_fill.reshape(batch)
    counts = [pltpu.SMEM((batch,), jnp.int32)] * 2
    fresh = [pltpu.VMEM(new_keys.shape, BF16)] * 2

    partials, held_keys, held_values = call(
        attention_kernel,
        "attention",
        [*map(in_hbm, (new_block, fill, queries, key_cache, value_cache, new_keys, new_values))],
        [ANY] * 7,
        (
            jax.ShapeDtypeStruct((heads_local * (batch + 2), head_dim), BF16),
            pltpu.VMEM(key_cache.shape, BF16),
            pltpu.VMEM(value_cache.shape, BF16),
        ),
        (VMEM, VMEM, VMEM),
        [
            *counts,
            pltpu.VMEM(queries.shape, BF16),
            *fresh,
            pltpu.VMEM((heads_local * (batch + 2), head_dim), F32),
            pltpu.SemaphoreType.DMA((7,)),
        ],
    )
    partials = partials.reshape(heads_local, batch // 2 + 1, 2, head_dim)
    gathered = lax.all_to_all(partials, SEQ, 0, 0).reshape(heads_local * (batch + 2), head_dim)
    heads = call(
        combine_kernel,
        "combine",
        [gathered],
        [VMEM],
        jax.ShapeDtypeStruct((devices, batch, head_dim), BF16),
        VMEM,
        [pltpu.VMEM((heads_local * (batch + 2), head_dim), F32)],
    )
    all_heads = lax.all_to_all(heads, ORDER, 0, 0)
    mixed, stream = call(
        project_kernel,
        "project",
        [all_heads, residual, norm_gain.reshape(1, columns), out_weight],
        [VMEM] * 4,
        (
            jax.ShapeDtypeStruct((batch, columns), F32),
            jax.ShapeDtypeStruct((devices // 8, 8 * (batch + 2), columns), BF16),
        ),
        (VMEM, VMEM),
    )
    stream = stream.reshape(devices, batch // 2 + 1, 2, columns)
    all_stream = lax.all_to_all(stream, ORDER, 0, 0)
    sums, keys_out, values_out = call(
        feed_kernel,
        "feed",
        [all_stream, gate_weight, up_weight, down_weight, held_keys, held_values],
        [VMEM] * 6,
        (
            jax.ShapeDtypeStruct((devices, batch, columns), BF16),
            jax.ShapeDtypeStruct(key_cache.shape, BF16),
            jax.ShapeDtypeStruct(value_cache.shape, BF16),
        ),
        (VMEM, ANY, ANY),
        [pltpu.SemaphoreType.DMA((2,))],
    )
    all_sums = lax.all_to_all(sums, ORDER, 0, 0)
    layer_out = call(
        finish_kernel,
        "finish",
        [all_sums, mixed],
        [VMEM] * 2,
        jax.ShapeDtypeStruct((batch, columns), BF16),
        VMEM,
    )
    return (layer_out, keys_out, values_out)


def solution(mesh):
    mesh = jax.sharding.Mesh(mesh.devices.reshape(SIZES), EVERY)
    placed = (
        P(None, "kvh", None),
        P(None, "kvh", SEQ, None),
        P(None, "kvh", SEQ, None),
        P(None, "kvh", None),
        P(None, "kvh", None),
        P(None, SEQ),
        P(),
        P(None, EVERY),
        P(EVERY),
        P(None, EVERY),
        P(EVERY, None),
        P(EVERY, None),
        P(EVERY, None),
    )
    return jax.shard_map(
        body,
        mesh=mesh,
        in_specs=placed,
        out_specs=(P(None, EVERY), P(None, "kvh", SEQ, None), P(None, "kvh", SEQ, None)),
        check_vma=False,
    )
```

```python
import functools

import jax
import jax.numpy as jnp
import numpy as np
from jax import lax
from jax.experimental import pallas as pl
from jax.experimental.pallas import tpu as pltpu
from jax.sharding import PartitionSpec as P

F32 = jnp.float32
BF16 = jnp.bfloat16
SEQ = ("y", "z", "core")
EVERY = ("kvh", "y", "z", "core")
SIZES = (4, 4, 4, 2)
ORDER = ("core", "z", "kvh", "y")
SLOT = np.arange(128).reshape(SIZES).transpose([EVERY.index(axis) for axis in ORDER]).reshape(-1).argsort().tolist()
VMEM = pl.BlockSpec(memory_space=pltpu.VMEM)
ANY = pl.BlockSpec(memory_space=pl.ANY)
MIB = 1 << 20
CHUNK = 2048
STEP = 256
COST = pl.CostEstimate(flops=20 * 10**9, bytes_accessed=60 * 10**6, transcendentals=20 * 10**6)


def nt_dot(a, b):
    return lax.dot_general(a, b, (((1,), (1,)), ((), ())), preferred_element_type=F32)


def tree_sum(terms):
    terms = list(terms)
    while len(terms) > 1:
        paired = [a + b for a, b in zip(terms[0::2], terms[1::2])]
        terms = paired + terms[len(paired) * 2 :]
    return terms[0]


def start_copies(pairs, sems, first=0):
    copies = [pltpu.make_async_copy(src, dst, sems.at[first + i]) for i, (src, dst) in enumerate(pairs)]
    for copy in copies:
        copy.start()
    return copies


def wait_copies(copies):
    for copy in copies:
        copy.wait()


def place_row(block, new_block, fill, new, cache):
    batch, kv_local, _, head_dim = cache.shape
    request = jnp.int32(-1)
    for b in range(batch):
        request = jnp.where(new_block[b] == block, b, request)

    @pl.when(request >= 0)
    def _():
        row = fill[request]
        start = pl.multiple_of((row // 16) * 16, 16)
        hit = lax.broadcasted_iota(jnp.int32, (16, head_dim), 0) == row - start
        for k in range(kv_local):
            old = cache[request, k, pl.ds(start, 16), :].astype(F32)
            fresh = new[request, k : k + 1, :].astype(F32)
            cache[request, k, pl.ds(start, 16), :] = jnp.where(hit, fresh, old).astype(BF16)


def attention_kernel(
    new_block_hbm,
    fill_hbm,
    queries_hbm,
    keys_hbm,
    values_hbm,
    new_keys_hbm,
    new_values_hbm,
    payload,
    keys,
    values,
    new_block,
    fill,
    queries,
    new_keys,
    new_values,
    rows_f32,
    sems,
):
    batch, heads_local, head_dim = queries.shape
    kv_local, rows = keys.shape[1], keys.shape[2]
    group = heads_local // kv_local
    block = (lax.axis_index("y") * lax.axis_size("z") + lax.axis_index("z")) * 2 + lax.axis_index("core")
    copies = start_copies(
        (
            (keys_hbm, keys),
            (queries_hbm, queries),
            (new_keys_hbm, new_keys),
            (new_block_hbm, new_block),
            (fill_hbm, fill),
            (values_hbm, values),
            (new_values_hbm, new_values),
        ),
        sems,
    )
    wait_copies(copies[:5])
    place_row(block, new_block, fill, new_keys, keys)

    lane = lax.broadcasted_iota(jnp.int32, (group, rows), 1)
    places = [(b, k) for b in range(batch) for k in range(kv_local)]
    live = [lane < fill[b] + jnp.where(new_block[b] == block, 1, 0) for b in range(batch)]
    scores = [nt_dot(queries[b, k * group : (k + 1) * group, :], keys[b, k]) for b, k in places]
    scores = [jnp.where(live[b], s * head_dim ** (-0.5), -1e30) for (b, _), s in zip(places, scores)]
    tops = [jnp.max(s, axis=1, keepdims=True).astype(BF16).astype(F32) for s in scores]
    weights = [
        jnp.where(live[b], jnp.exp(s - t), 0.0).astype(BF16) for (b, _), s, t in zip(places, scores, tops)
    ]
    totals = [jnp.sum(w.astype(F32), axis=1, keepdims=True) for w in weights]
    wait_copies(copies[5:])
    place_row(block, new_block, fill, new_values, values)
    sums = [jnp.dot(w, values[b, k], preferred_element_type=F32) for (b, k), w in zip(places, weights)]
    height = batch + 2
    for (b, k), summed in zip(places, sums):
        rows_f32[pl.ds(k * group * height + b, group, stride=height), :] = summed
    for k in range(kv_local):
        first = jnp.zeros(lane.shape, F32)
        second = jnp.zeros(lane.shape, F32)
        for b in range(batch):
            top, total = tops[b * kv_local + k], totals[b * kv_local + k]
            high = total.astype(BF16).astype(F32)
            first = jnp.where(lane == b, top, jnp.where(lane == 64 + b, high, first))
            second = jnp.where(lane == b, total - high, second)
        rows_f32[pl.ds(k * group * height + batch, group, stride=height), :] = first
        rows_f32[pl.ds(k * group * height + batch + 1, group, stride=height), :] = second
    payload[...] = rows_f32[...].astype(BF16)


def combine_kernel(parts, out, rows):
    batch = out.shape[1]
    height = batch + 2
    sources = parts.shape[0] // height
    rows[...] = parts[...].astype(F32)
    first = rows[pl.ds(batch, sources, stride=height), :]
    second = rows[pl.ds(batch + 1, sources, stride=height), :]
    total = pltpu.roll(first, 64, 1) + second
    weights = jnp.exp(jnp.minimum(first - jnp.max(first, axis=0, keepdims=True), 0.0))
    scale = weights / jnp.sum(weights * total, axis=0, keepdims=True)
    heads = jnp.concatenate(
        [
            jnp.sum(rows[pl.ds(b, sources, stride=height), :] * scale[:, b : b + 1], axis=0, keepdims=True)
            for b in range(batch)
        ],
        axis=0,
    ).astype(BF16)
    for p in range(out.shape[0]):
        out[p] = heads


def project_kernel(heads, residual, gain, weight, mixed_out, payload):
    per = CHUNK // 128
    total = residual[...] + tree_sum(
        jnp.dot(
            jnp.concatenate([heads[SLOT[c * per + i]] for i in range(per)], axis=1),
            weight[c * CHUNK : (c + 1) * CHUNK, :],
            preferred_element_type=F32,
        )
        for c in range(weight.shape[0] // CHUNK)
    )
    mixed_out[...] = total
    square = jnp.sum(total * total, axis=1, keepdims=True)
    high = square.astype(BF16).astype(F32)
    low = square - high
    lane = lax.broadcasted_iota(jnp.int32, (2, total.shape[1]), 1)
    stats = jnp.zeros(lane.shape, F32)
    for b in range(total.shape[0]):
        stats = jnp.where(lane == b, high[b : b + 1], jnp.where(lane == 64 + b, low[b : b + 1], stats))
    tile = jnp.concatenate([total * gain[...], stats], axis=0).astype(BF16)
    whole = jnp.concatenate([tile] * (payload.shape[1] // tile.shape[0]), axis=0)
    for p in range(payload.shape[0]):
        payload[p] = whole


def feed_kernel(tiles, gate, up, down, keys, values, out, keys_out, values_out, sems):
    writes = start_copies(((keys, keys_out), (values, values_out)), sems)
    features = gate.shape[1]
    squares = tree_sum(tiles[p, 4].astype(F32) for p in range(tiles.shape[0]))
    squares = squares + pltpu.roll(squares, 64, 1)
    factor = jnp.concatenate([lax.rsqrt(squares[0:1, b : b + 1] / features + 1e-05) for b in range(8)], axis=0)
    gate_sum = 0.0
    up_sum = 0.0
    for c in range(features // STEP):
        first = c * STEP // 128
        piece = jnp.concatenate(
            [
                jnp.concatenate([tiles[SLOT[first + i], j] for j in range(tiles.shape[1] - 1)], axis=0)
                for i in range(STEP // 128)
            ],
            axis=1,
        )
        part = slice(c * STEP, (c + 1) * STEP)
        gate_sum = gate_sum + nt_dot(gate[:, part], piece)
        up_sum = up_sum + nt_dot(piece, up[:, part])
    gate_sum = gate_sum.T * factor
    up_sum = up_sum * factor
    hidden = (gate_sum / (1.0 + jnp.exp(-gate_sum)) * up_sum).astype(BF16)
    per = CHUNK // 128
    for c in range(features // CHUNK):
        sums = jnp.dot(hidden, down[:, c * CHUNK : (c + 1) * CHUNK], preferred_element_type=F32).astype(BF16)
        for i in range(per):
            out[SLOT[c * per + i]] = sums[:, i * 128 : (i + 1) * 128]
    wait_copies(writes)


def finish_kernel(sums, mixed, out):
    total = tree_sum(sums[p].astype(F32) for p in range(sums.shape[0]))
    out[...] = (mixed[...] + total).astype(BF16)


def in_hbm(x):
    return pltpu.with_memory_space_constraint(x, pltpu.HBM)


def call(kernel, name, operands, in_specs, out_shape, out_specs, scratch=()):
    return pl.pallas_call(
        kernel,
        out_shape=out_shape,
        in_specs=in_specs,
        out_specs=out_specs,
        scratch_shapes=list(scratch),
        compiler_params=pltpu.CompilerParams(vmem_limit_bytes=4 * MIB),
        cost_estimate=COST,
        name=name,
    )(*operands)


def body(
    queries,
    key_cache,
    value_cache,
    new_keys,
    new_values,
    block_fill,
    new_block,
    residual,
    norm_gain,
    out_weight,
    gate_weight,
    up_weight,
    down_weight,
):
    batch, heads_local, head_dim = queries.shape
    devices = lax.axis_size(EVERY)
    columns = residual.shape[1]
    fill = block_fill.reshape(batch)
    counts = [pltpu.SMEM((batch,), jnp.int32)] * 2
    fresh = [pltpu.VMEM(new_keys.shape, BF16)] * 2

    partials, held_keys, held_values = call(
        attention_kernel,
        "attention",
        [*map(in_hbm, (new_block, fill, queries, key_cache, value_cache, new_keys, new_values))],
        [ANY] * 7,
        (
            jax.ShapeDtypeStruct((heads_local * (batch + 2), head_dim), BF16),
            pltpu.VMEM(key_cache.shape, BF16),
            pltpu.VMEM(value_cache.shape, BF16),
        ),
        (VMEM, VMEM, VMEM),
        [
            *counts,
            pltpu.VMEM(queries.shape, BF16),
            *fresh,
            pltpu.VMEM((heads_local * (batch + 2), head_dim), F32),
            pltpu.SemaphoreType.DMA((7,)),
        ],
    )
    partials = partials.reshape(heads_local, batch // 2 + 1, 2, head_dim)
    gathered = lax.all_to_all(partials, SEQ, 0, 0).reshape(heads_local * (batch + 2), head_dim)
    heads = call(
        combine_kernel,
        "combine",
        [gathered],
        [VMEM],
        jax.ShapeDtypeStruct((devices, batch, head_dim), BF16),
        VMEM,
        [pltpu.VMEM((heads_local * (batch + 2), head_dim), F32)],
    )
    all_heads = lax.all_to_all(heads, ORDER, 0, 0)
    mixed, stream = call(
        project_kernel,
        "project",
        [all_heads, residual, norm_gain.reshape(1, columns), out_weight],
        [VMEM] * 4,
        (
            jax.ShapeDtypeStruct((batch, columns), F32),
            jax.ShapeDtypeStruct((devices // 8, 8 * (batch + 2), columns), BF16),
        ),
        (VMEM, VMEM),
    )
    stream = stream.reshape(devices, batch // 2 + 1, 2, columns)
    all_stream = lax.all_to_all(stream, ORDER, 0, 0)
    sums, keys_out, values_out = call(
        feed_kernel,
        "feed",
        [all_stream, gate_weight, up_weight, down_weight, held_keys, held_values],
        [VMEM] * 6,
        (
            jax.ShapeDtypeStruct((devices, batch, columns), BF16),
            jax.ShapeDtypeStruct(key_cache.shape, BF16),
            jax.ShapeDtypeStruct(value_cache.shape, BF16),
        ),
        (VMEM, ANY, ANY),
        [pltpu.SemaphoreType.DMA((2,))],
    )
    all_sums = lax.all_to_all(sums, ORDER, 0, 0)
    layer_out = call(
        finish_kernel,
        "finish",
        [all_sums, mixed],
        [VMEM] * 2,
        jax.ShapeDtypeStruct((batch, columns), BF16),
        VMEM,
    )
    return (layer_out, keys_out, values_out)


def solution(mesh):
    mesh = jax.sharding.Mesh(mesh.devices.reshape(SIZES), EVERY)
    placed = (
        P(None, "kvh", None),
        P(None, "kvh", SEQ, None),
        P(None, "kvh", SEQ, None),
        P(None, "kvh", None),
        P(None, "kvh", None),
        P(None, SEQ),
        P(),
        P(None, EVERY),
        P(EVERY),
        P(None, EVERY),
        P(EVERY, None),
        P(EVERY, None),
        P(EVERY, None),
    )
    return jax.shard_map(
        body,
        mesh=mesh,
        in_specs=placed,
        out_specs=(P(None, EVERY), P(None, "kvh", SEQ, None), P(None, "kvh", SEQ, None)),
        check_vma=False,
    )
```
